512 devices in a mesh: dp: 16 (over x, z_lo), work: 32 (over y, z_hi, core).
Axes of the slice: x: 4, y: 4, z: 16 (z_hi: 4, z_lo: 4; z = z_hi * 4 + z_lo), core: 2. Of those that a mesh axis runs over, the one named last changes fastest.
Arguments:
- activations: bfloat16 [16384, 4096], P('dp', 'work'), may hold values from -6 to 6
- gradients: bfloat16 [16384, 8192], P('dp', 'work'), may hold values from -0.125 to 0.125
- left_panels: bfloat16 [32, 1024, 128], P('work'), may hold values from -1 to 2
- panel_slot: int32 [32], replicated, may hold values from 0 to 31, as said below
- right_inverse: bfloat16 [1024, 8192], P(None, 'work'), may hold values from -1 to 2
Outputs:
- input_factor: float32 [1024, 4096], P(None, 'work')
- output_factor: float32 [1024, 8192], P(None, 'work')
- step_update: bfloat16 [4096, 8192], P('dp', 'work')
The draws below stay inside these ranges and needn't reach their ends.
Inputs may be any that keep to these rules, and one draw needn't show every extreme that they name: `panel_slot`: each slot number appears once.
All inputs are finite; a program needn't handle non-finite values.
Results may differ from the reference program's by a relative error of at most 0.018.
Values may be sent and summed in bfloat16 or wider, within the bound.
No kernel may reach another device: no remote copies, remote signals or barrier semaphores. Data moves between devices by JAX's collectives and lax.ppermute only.
A program may use at most 64 MiB of HBM per device.

```python
import jax
import jax.numpy as jnp
from jax import lax

D = 4096
FFW = 8192
BLK = 1024
PW = 128
TOKENS = 16384
NPAN = 32


def slot_order(key):
    return jax.random.permutation(jax.random.fold_in(key, 5), NPAN).astype(jnp.int32)


def draw_panel_slot(key, part):
    return slot_order(key)


def draw_left_panels(key, part):
    order = slot_order(key)
    key = jax.random.fold_in(key, 2)
    holder = jnp.argsort(order)
    within = holder % (BLK // PW)
    row_ids = jnp.arange(BLK)[None, :, None]
    col_ids = jnp.arange(PW)[None, None, :]
    diagonal = (row_ids == within[:, None, None] * PW + col_ids).astype(jnp.float32)
    noise = jax.random.uniform(key, (NPAN, BLK, PW), jnp.float32, -1.0, 1.0)
    return (diagonal + noise * (1.5 / BLK ** 0.5)).astype(jnp.bfloat16)


def draw_right_inverse(key, part):
    key = jax.random.fold_in(key, 3)
    row_ids = jnp.arange(BLK)[:, None]
    col_ids = jnp.arange(FFW)[None, :]
    diagonal = (row_ids == col_ids % BLK).astype(jnp.float32)
    noise = jax.random.uniform(key, (BLK, FFW), jnp.float32, -1.0, 1.0)
    return (diagonal + noise * (1.5 / BLK ** 0.5)).astype(jnp.bfloat16)


def shard_levels(own_key, dims, cuts, smallest, top_value):
    level, own = 1.0, jax.random.fold_in(own_key, 6)
    for position, blocks in cuts:
        draws = jnp.exp(jax.random.uniform(jax.random.fold_in(own, position), (blocks,), jnp.float32, smallest / len(cuts), top_value / len(cuts)))
        level = level * jnp.repeat(draws, dims[position] // blocks).reshape([-1 if axis == position else 1 for axis in range(len(dims))])
    return level


def normal_values(key, shape, width, limit, pieces=(), held_as=jnp.bfloat16):
    result = width * jax.random.normal(key, shape, jnp.float32)
    if pieces:
        result = result * shard_levels(key, shape, pieces, -0.22, 0.18)
    return jnp.clip(result, -limit, limit).astype(held_as)


def setup_inputs(seed: int = 0) -> dict:
    key_of = jax.random.split(jax.random.key(seed), 6)
    activations = normal_values(key_of[0], (TOKENS, D), 1.0, 6.0, ((0, 16), (1, 32)))
    gradients = normal_values(key_of[1], (TOKENS, FFW), (TOKENS ** -0.5), 0.125, ((0, 16), (1, 32)))
    left_panels = draw_left_panels(jax.random.fold_in(key_of[5], 71), 0)
    panel_slot = draw_panel_slot(jax.random.fold_in(key_of[5], 71), 0)
    right_inverse = draw_right_inverse(jax.random.fold_in(key_of[5], 71), 0)
    return {"activations": activations, "gradients": gradients, "left_panels": left_panels, "panel_slot": panel_slot, "right_inverse": right_inverse}


def reference(activations, gradients, left_panels, panel_slot, right_inverse):
    a_blocks = D // BLK
    g_blocks = FFW // BLK
    act_wide = activations.astype(jnp.float32).reshape(TOKENS, a_blocks, BLK)
    input_factor = jnp.einsum("tbj,tbr->jbr", act_wide, act_wide, precision=lax.Precision.HIGHEST).reshape(BLK, D) / TOKENS
    grad_wide = gradients.astype(jnp.float32).reshape(TOKENS, g_blocks, BLK)
    output_factor = jnp.einsum("tbj,tbr->jbr", grad_wide, grad_wide, precision=lax.Precision.HIGHEST).reshape(BLK, FFW)
    weight_grad = jnp.dot(activations.T, gradients, preferred_element_type=jnp.float32)
    right_wide = jnp.einsum("rcj,jcf->rcf", weight_grad.reshape(D, g_blocks, BLK), right_inverse.astype(jnp.float32).reshape(BLK, g_blocks, BLK), precision=lax.Precision.HIGHEST)
    right_side = right_wide.reshape(D, FFW).astype(jnp.bfloat16)
    left_factor = jnp.transpose(left_panels[panel_slot], (1, 0, 2)).reshape(BLK, D)
    step_update = jnp.einsum("jbr,bjf->brf", left_factor.astype(jnp.float32).reshape(BLK, a_blocks, BLK), right_side.astype(jnp.float32).reshape(a_blocks, BLK, FFW), precision=lax.Precision.HIGHEST)
    step_update = step_update.reshape(D, FFW).astype(jnp.bfloat16)
    return input_factor, output_factor, step_update
```

```python
import jax
import jax.numpy as jnp
import numpy as np
from jax import lax
from jax.sharding import Mesh, PartitionSpec as P

BF16 = jnp.bfloat16
SHIFTS = (1, 2, 3)


def shifted(value, axis, shift):
    size = lax.axis_size(axis)
    return lax.ppermute(value, axis, [(i, (i + shift) % size) for i in range(size)])


def swapped(value, axis, mask):
    return lax.ppermute(value, axis, [(i, i ^ mask) for i in range(lax.axis_size(axis))])


def contract_rows(first_operand, second_operand):
    return lax.dot_general(
        first_operand, second_operand, (((0,), (0,)), ((), ())), preferred_element_type=jnp.float32
    )


def pick(stacked, index):
    return lax.dynamic_index_in_dim(stacked, index, 0, keepdims=False)


def contract_tokens(stacked, values):
    return jnp.einsum("btf,tc->bfc", stacked, values, preferred_element_type=jnp.float32)


def product(values, matrix):
    return jnp.dot(values, matrix, preferred_element_type=jnp.float32)


def block_order(values, place, levels):
    columns = values.shape[-1]
    values = values.reshape((2,) * levels + (-1, columns))
    for level in range(levels):
        flipped = jnp.flip(values, levels - 1 - level)
        values = jnp.where((place >> level) % 2 == 1, flipped, values)
    return values.reshape(-1, columns)


def together(*values):
    return lax.optimization_barrier(values)


def after(value, *others):
    return together(value, *others)[0]


def exchanged(pieces, axes):
    return lax.all_to_all(pieces, axes, 0, 0, tiled=True)


def to_all(value, axes, members):
    return exchanged(jnp.broadcast_to(value[None], (members,) + value.shape), axes)


def block_panels(side, panel_slot, h, k):
    rows, width = side.shape[1] // 8, side.shape[2]
    side = side.reshape(16, 2, rows, width)
    own = lax.dynamic_index_in_dim(side, k, 1, keepdims=False)
    other = swapped(lax.dynamic_index_in_dim(side, 1 - k, 1, keepdims=False), "k", 1)
    stored = jnp.concatenate([own, other], 0)
    at = (panel_slot // 2 ^ h) + 16 * ((panel_slot + k) % 2)
    ordered = jnp.take(stored, at, axis=0, mode="clip")
    return ordered.reshape(4, 8, rows, width)


def local(activations, gradients, left_panels, panel_slot, right_inverse):
    x, l, h, k = (lax.axis_index(name) for name in ("x", "l", "h", "k"))
    total_tokens = activations.shape[0] * 16
    tokens, width = gradients.shape
    own_width = activations.shape[1]
    place = 2 * (h % 2) + k

    panel = pick(left_panels.reshape(4, -1, own_width), x)
    act_0 = jnp.concatenate([activations, panel], 0)
    act_1 = swapped(act_0, "h", 1)
    act_3 = swapped(act_0, "h", 3)
    panel_2 = swapped(panel, "h", 2)
    act_1, act_3, panel_2, gradients = together(act_1, act_3, panel_2, gradients)
    act_2 = swapped(act_1[:tokens], "h", 3)
    grad_1 = swapped(gradients, "h", 1)
    panels = jnp.concatenate([panel, act_1[tokens:], panel_2, act_3[tokens:]], 0)
    mine = jnp.concatenate([activations, act_1[:tokens], act_3[:tokens], panels], 1)
    early = to_all(mine, "y", 4)
    grad_other = swapped(gradients, "k", 1)
    mine_other = swapped(mine, "k", 1)
    inverse = block_order(right_inverse, place, 2).reshape(4, width, -1)
    grad_right = product(gradients, inverse[0]) + product(grad_other, inverse[1])
    output_part = [contract_rows(gradients, gradients), contract_rows(grad_other, gradients)]
    input_part = [contract_rows(part, activations) for part in (mine, mine_other)]
    act_2, grad_1, early, grad_right, inverse, output_0, output_1, input_0, input_1 = together(
        act_2, grad_1, early, grad_right, inverse, *output_part, *input_part
    )

    third = to_all(act_2, "y", 4)
    grad_1_other = swapped(grad_1, "k", 1)
    grad_right = grad_right + product(grad_1, inverse[2]) + product(grad_1_other, inverse[3])
    grad_right = grad_right.astype(BF16)
    ordered = block_panels(early[..., 3 * own_width :], panel_slot, h, k)
    grad_right_other, ordered = together(swapped(grad_right, "k", 1), ordered)
    grad_right = jnp.concatenate([grad_right, grad_right_other], 1)

    terms = contract_tokens(early, grad_right)[:, : 3 * own_width]
    terms = jnp.concatenate([terms, contract_tokens(third, grad_right)], 1)
    terms, act_2, grad_1 = together(terms.astype(BF16), act_2, grad_1)
    got = exchanged(terms, "x")

    input_part = [
        jnp.concatenate([part[: 3 * own_width], contract_rows(last, activations)], 0)
        for part, last in ((input_0, act_2), (input_1, swapped(act_2, "k", 1)))
    ]
    input_part = jnp.stack([part.reshape(4, own_width, own_width) for part in input_part], 1)
    input_part = jnp.concatenate([input_part[:2], input_part[3:], input_part[2:3]], 0)
    input_part = block_order(input_part, 2 * h + k, 3)
    output_part = [output_0, output_1, contract_rows(grad_1, gradients)]
    output_part = jnp.stack(output_part + [contract_rows(grad_1_other, gradients)])
    output_part = block_order(output_part, place, 2)
    factors = jnp.concatenate([input_part, output_part], 1).astype(BF16)
    factors = factors.reshape(4, -1, factors.shape[1])
    quarter = pick(factors, l).astype(jnp.float32)
    for shift in SHIFTS:
        sent = pick(factors, (l + shift) % 4)
        quarter = quarter + shifted(sent, "l", shift).astype(jnp.float32)
    quarter = quarter.astype(BF16)

    rows_got = [pick(ordered, x)] + [shifted(pick(ordered, (x + s) % 4), "x", s) for s in SHIFTS]
    got, quarter, *rows_got = together(got, quarter, *rows_got)
    rows_got = jnp.stack(rows_got)
    left = jnp.concatenate([pick(rows_got, (x - (h ^ m)) % 4) for m in (0, 1, 3, 2)], 1)
    left_other = swapped(left, "k", 1)

    quarter = jnp.sum(to_all(quarter, "x", 4).astype(jnp.float32), 0).astype(BF16)
    right_rows = jnp.sum(got.astype(jnp.float32), 0).astype(BF16)
    right_other = swapped(right_rows[:, width:], "k", 1)
    update = contract_tokens(left, right_rows[:, :width]) + contract_tokens(left_other, right_other)
    update = update.astype(BF16).reshape(4, -1, width)
    quarter = jnp.broadcast_to(quarter[None], (4,) + quarter.shape)
    joint = exchanged(jnp.concatenate([update, quarter], 2), "l")
    step_update = jnp.sum(joint[..., :width].astype(jnp.float32), 0).astype(BF16)
    factors = joint[..., width:].reshape(-1, quarter.shape[2]).astype(jnp.float32)
    return factors[:, :own_width] / total_tokens, factors[:, own_width:], step_update


def solution(mesh):
    whole = Mesh(np.asarray(mesh.devices).reshape(4, 4, 4, 4, 2), ("x", "l", "y", "h", "k"))
    dp, work = ("x", "l"), ("y", "h", "k")
    return jax.shard_map(
        local,
        mesh=whole,
        in_specs=(P(dp, work), P(dp, work), P(work, None, None), P(), P(None, work)),
        out_specs=(P(None, work), P(None, work), P(dp, work)),
        check_vma=False,
    )
```

```python
import jax
import jax.numpy as jnp
import numpy as np
from jax import lax
from jax.sharding import Mesh, PartitionSpec as P

BF16 = jnp.bfloat16
SHIFTS = (1, 2, 3)


def shifted(value, axis, shift):
    size = lax.axis_size(axis)
    return lax.ppermute(value, axis, [(i, (i + shift) % size) for i in range(size)])


def swapped(value, axis, mask):
    return lax.ppermute(value, axis, [(i, i ^ mask) for i in range(lax.axis_size(axis))])


def contract_rows(first_operand, second_operand):
    return lax.dot_general(
        first_operand, second_operand, (((0,), (0,)), ((), ())), preferred_element_type=jnp.float32
    )


def pick(stacked, index):
    return lax.dynamic_index_in_dim(stacked, index, 0, keepdims=False)


def contract_tokens(stacked, values):
    return jnp.einsum("btf,tc->bfc", stacked, values, preferred_element_type=jnp.float32)


def product(values, matrix):
    return jnp.dot(values, matrix, preferred_element_type=jnp.float32)


def block_order(values, place, levels):
    columns = values.shape[-1]
    values = values.reshape((2,) * levels + (-1, columns))
    for level in range(levels):
        flipped = jnp.flip(values, levels - 1 - level)
        values = jnp.where((place >> level) % 2 == 1, flipped, values)
    return values.reshape(-1, columns)


def together(*values):
    return lax.optimization_barrier(values)


def after(value, *others):
    return together(value, *others)[0]


def exchanged(pieces, axes):
    return lax.all_to_all(pieces, axes, 0, 0, tiled=True)


def to_all(value, axes, members):
    return exchanged(jnp.broadcast_to(value[None], (members,) + value.shape), axes)


def block_panels(side, panel_slot, h, k):
    rows, width = side.shape[1] // 8, side.shape[2]
    side = side.reshape(16, 2, rows, width)
    own = lax.dynamic_index_in_dim(side, k, 1, keepdims=False)
    other = swapped(lax.dynamic_index_in_dim(side, 1 - k, 1, keepdims=False), "k", 1)
    stored = jnp.concatenate([own, other], 0)
    at = (panel_slot // 2 ^ h) + 16 * ((panel_slot + k) % 2)
    ordered = jnp.take(stored, at, axis=0, mode="clip")
    return ordered.reshape(4, 8, rows, width)


def local(activations, gradients, left_panels, panel_slot, right_inverse):
    x, l, h, k = (lax.axis_index(name) for name in ("x", "l", "h", "k"))
    total_tokens = activations.shape[0] * 16
    tokens, width = gradients.shape
    own_width = activations.shape[1]
    place = 2 * (h % 2) + k

    panel = pick(left_panels.reshape(4, -1, own_width), x)
    act_0 = jnp.concatenate([activations, panel], 0)
    act_1 = swapped(act_0, "h", 1)
    act_3 = swapped(act_0, "h", 3)
    act_1, act_3, gradients = together(act_1, act_3, gradients)
    act_2 = swapped(act_1, "h", 3)
    grad_1 = swapped(gradients, "h", 1)
    panels = jnp.concatenate([panel, act_1[tokens:], panel, act_3[tokens:]], 0)
    mine = jnp.concatenate([activations, act_1[:tokens], act_3[:tokens], panels], 1)
    early = to_all(mine, "y", 4)
    grad_other = swapped(gradients, "k", 1)
    mine_other = swapped(mine, "k", 1)
    inverse = block_order(right_inverse, place, 2).reshape(4, width, -1)
    grad_right = product(gradients, inverse[0]) + product(grad_other, inverse[1])
    output_part = [contract_rows(gradients, gradients), contract_rows(grad_other, gradients)]
    input_part = [contract_rows(part, activations) for part in (mine, mine_other)]
    act_2, grad_1, early, grad_right, inverse, output_0, output_1, input_0, input_1 = together(
        act_2, grad_1, early, grad_right, inverse, *output_part, *input_part
    )

    third = to_all(act_2, "y", 4)
    grad_1_other = swapped(grad_1, "k", 1)
    grad_right = grad_right + product(grad_1, inverse[2]) + product(grad_1_other, inverse[3])
    grad_right = grad_right.astype(BF16)
    grad_right = jnp.concatenate([grad_right, swapped(grad_right, "k", 1)], 1)

    terms = contract_tokens(early, grad_right)[:, : 3 * own_width]
    terms = jnp.concatenate([terms, contract_tokens(third[:, :tokens], grad_right)], 1)
    terms, act_2, grad_1, early, third = together(
        terms.astype(BF16), act_2[:tokens], grad_1, early, third
    )
    got = exchanged(terms, "x")

    input_part = [
        jnp.concatenate([part[: 3 * own_width], contract_rows(last, activations)], 0)
        for part, last in ((input_0, act_2), (input_1, swapped(act_2, "k", 1)))
    ]
    input_part = jnp.stack([part.reshape(4, own_width, own_width) for part in input_part], 1)
    input_part = jnp.concatenate([input_part[:2], input_part[3:], input_part[2:3]], 0)
    input_part = block_order(input_part, 2 * h + k, 3)
    output_part = [output_0, output_1, contract_rows(grad_1, gradients)]
    output_part = jnp.stack(output_part + [contract_rows(grad_1_other, gradients)])
    output_part = block_order(output_part, place, 2)
    factors = jnp.concatenate([input_part, output_part], 1).astype(BF16)
    factors = factors.reshape(4, -1, factors.shape[1])
    quarter = pick(factors, l).astype(jnp.float32)
    for shift in SHIFTS:
        sent = pick(factors, (l + shift) % 4)
        quarter = quarter + shifted(sent, "l", shift).astype(jnp.float32)
    quarter = quarter.astype(BF16)

    held = panel.shape[0]
    side = early[..., 3 * own_width :]
    side = jnp.concatenate([side[:, : 2 * held], third[:, tokens:], side[:, 3 * held :]], 1)
    ordered = block_panels(side, panel_slot, h, k)
    rows_got = [pick(ordered, x)] + [shifted(pick(ordered, (x + s) % 4), "x", s) for s in SHIFTS]
    got, quarter, *rows_got = together(got, quarter, *rows_got)
    rows_got = jnp.stack(rows_got)
    left = jnp.concatenate([pick(rows_got, (x - (h ^ m)) % 4) for m in (0, 1, 3, 2)], 1)
    left_other = swapped(left, "k", 1)

    quarter = jnp.sum(to_all(quarter, "x", 4).astype(jnp.float32), 0).astype(BF16)
    right_rows = jnp.sum(got.astype(jnp.float32), 0).astype(BF16)
    right_other = swapped(right_rows[:, width:], "k", 1)
    update = contract_tokens(left, right_rows[:, :width]) + contract_tokens(left_other, right_other)
    update = update.astype(BF16).reshape(4, -1, width)
    quarter = jnp.broadcast_to(quarter[None], (4,) + quarter.shape)
    joint = exchanged(jnp.concatenate([update, quarter], 2), "l")
    step_update = jnp.sum(joint[..., :width].astype(jnp.float32), 0).astype(BF16)
    factors = joint[..., width:].reshape(-1, quarter.shape[2]).astype(jnp.float32)
    return factors[:, :own_width] / total_tokens, factors[:, own_width:], step_update


def solution(mesh):
    whole = Mesh(np.asarray(mesh.devices).reshape(4, 4, 4, 4, 2), ("x", "l", "y", "h", "k"))
    dp, work = ("x", "l"), ("y", "h", "k")
    return jax.shard_map(
        local,
        mesh=whole,
        in_specs=(P(dp, work), P(dp, work), P(work, None, None), P(), P(None, work)),
        out_specs=(P(None, work), P(None, work), P(dp, work)),
        check_vma=False,
    )
```

```python
import jax
import jax.numpy as jnp
import numpy as np
from jax import lax
from jax.sharding import Mesh, PartitionSpec as P

BF16 = jnp.bfloat16
SHIFTS = (1, 2, 3)


def shifted(value, axis, shift):
    size = lax.axis_size(axis)
    return lax.ppermute(value, axis, [(i, (i + shift) % size) for i in range(size)])


def swapped(value, axis, mask):
    return lax.ppermute(value, axis, [(i, i ^ mask) for i in range(lax.axis_size(axis))])


def contract_rows(first_operand, second_operand):
    return lax.dot_general(
        first_operand, second_operand, (((0,), (0,)), ((), ())), preferred_element_type=jnp.float32
    )


def pick(stacked, index):
    return lax.dynamic_index_in_dim(stacked, index, 0, keepdims=False)


def contract_tokens(stacked, values):
    return jnp.einsum("btf,tc->bfc", stacked, values, preferred_element_type=jnp.float32)


def product(values, matrix):
    return jnp.dot(values, matrix, preferred_element_type=jnp.float32)


def block_order(values, place, levels):
    columns = values.shape[-1]
    values = values.reshape((2,) * levels + (-1, columns))
    for level in range(levels):
        flipped = jnp.flip(values, levels - 1 - level)
        values = jnp.where((place >> level) % 2 == 1, flipped, values)
    return values.reshape(-1, columns)


def together(*values):
    return lax.optimization_barrier(values)


def after(value, *others):
    return together(value, *others)[0]


def exchanged(pieces, axes):
    return lax.all_to_all(pieces, axes, 0, 0, tiled=True)


def to_all(value, axes, members):
    return exchanged(jnp.broadcast_to(value[None], (members,) + value.shape), axes)


def block_panels(side, panel_slot, h, k):
    rows, width = side.shape[1] // 8, side.shape[2]
    side = side.reshape(16, 2, rows, width)
    own = lax.dynamic_index_in_dim(side, k, 1, keepdims=False)
    other = swapped(lax.dynamic_index_in_dim(side, 1 - k, 1, keepdims=False), "k", 1)
    stored = jnp.concatenate([own, other], 0)
    at = (panel_slot // 2 ^ h) + 16 * ((panel_slot + k) % 2)
    ordered = jnp.take(stored, at, axis=0, mode="clip")
    return ordered.reshape(4, 8, rows, width)


def local(activations, gradients, left_panels, panel_slot, right_inverse):
    x, l, h, k = (lax.axis_index(name) for name in ("x", "l", "h", "k"))
    total_tokens = activations.shape[0] * 16
    tokens, width = gradients.shape
    own_width = activations.shape[1]
    place = 2 * (h % 2) + k

    panel = pick(left_panels.reshape(4, -1, own_width), x)
    act_0 = jnp.concatenate([activations, panel], 0)
    act_1 = swapped(act_0, "h", 1)
    act_3 = swapped(act_0, "h", 3)
    act_1, act_3, gradients = together(act_1, act_3, gradients)
    act_2 = swapped(act_1, "h", 3)
    grad_1 = swapped(gradients, "h", 1)
    panels = jnp.concatenate([panel, act_1[tokens:], panel, act_3[tokens:]], 0)
    mine = jnp.concatenate([activations, act_1[:tokens], act_3[:tokens], panels], 1)
    early = to_all(mine, "y", 4)
    grad_other = swapped(gradients, "k", 1)
    mine_other = swapped(mine, "k", 1)
    inverse = block_order(right_inverse, place, 2).reshape(4, width, -1)
    grad_right = product(gradients, inverse[0]) + product(grad_other, inverse[1])
    output_part = [contract_rows(gradients, gradients), contract_rows(grad_other, gradients)]
    input_part = [contract_rows(part, activations) for part in (mine, mine_other)]
    act_2, grad_1, early, grad_right, inverse, output_0, output_1, input_0, input_1 = together(
        act_2, grad_1, early, grad_right, inverse, *output_part, *input_part
    )

    third = to_all(act_2, "y", 4)
    grad_1_other = swapped(grad_1, "k", 1)
    grad_right = grad_right + product(grad_1, inverse[2]) + product(grad_1_other, inverse[3])
    grad_right = grad_right.astype(BF16)
    grad_right = jnp.concatenate([grad_right, swapped(grad_right, "k", 1)], 1)

    terms = contract_tokens(early, grad_right)[:, : 3 * own_width]
    terms = jnp.concatenate([terms, contract_tokens(third[:, :tokens], grad_right)], 1)
    terms, act_2, grad_1, early, third = together(
        terms.astype(BF16), act_2[:tokens], grad_1, early, third
    )
    got = exchanged(terms, "x")

    input_part = [
        jnp.concatenate([part[: 3 * own_width], contract_rows(last, activations)], 0)
        for part, last in ((input_0, act_2), (input_1, swapped(act_2, "k", 1)))
    ]
    input_part = jnp.stack([part.reshape(4, own_width, own_width) for part in input_part], 1)
    input_part = jnp.concatenate([input_part[:2], input_part[3:], input_part[2:3]], 0)
    input_part = block_order(input_part, 2 * h + k, 3)
    output_part = [output_0, output_1, contract_rows(grad_1, gradients)]
    output_part = jnp.stack(output_part + [contract_rows(grad_1_other, gradients)])
    output_part = block_order(output_part, place, 2)
    factors = jnp.concatenate([input_part, output_part], 1).astype(BF16)
    factors = factors.reshape(4, -1, factors.shape[1])
    quarter = pick(factors, l).astype(jnp.float32)
    for shift in SHIFTS:
        sent = pick(factors, (l + shift) % 4)
        quarter = quarter + shifted(sent, "l", shift).astype(jnp.float32)
    quarter = quarter.astype(BF16)

    held = panel.shape[0]
    side = early[..., 3 * own_width :]
    side = jnp.concatenate([side[:, : 2 * held], third[:, tokens:], side[:, 3 * held :]], 1)
    ordered = block_panels(side, panel_slot, h, k)
    rows_got = [pick(ordered, x)] + [shifted(pick(ordered, (x + s) % 4), "x", s) for s in SHIFTS]
    rows_got = jnp.stack(rows_got)
    left = jnp.concatenate([pick(rows_got, (x - (h ^ m)) % 4) for m in (0, 1, 3, 2)], 1)
    left_other = swapped(left, "k", 1)

    quarter = jnp.sum(to_all(quarter, "x", 4).astype(jnp.float32), 0).astype(BF16)
    right_rows = jnp.sum(got.astype(jnp.float32), 0).astype(BF16)
    right_other = swapped(right_rows[:, width:], "k", 1)
    update = contract_tokens(left, right_rows[:, :width]) + contract_tokens(left_other, right_other)
    update = update.astype(BF16).reshape(4, -1, width)
    quarter = jnp.broadcast_to(quarter[None], (4,) + quarter.shape)
    joint = exchanged(jnp.concatenate([update, quarter], 2), "l")
    step_update = jnp.sum(joint[..., :width].astype(jnp.float32), 0).astype(BF16)
    factors = joint[..., width:].reshape(-1, quarter.shape[2]).astype(jnp.float32)
    return factors[:, :own_width] / total_tokens, factors[:, own_width:], step_update


def solution(mesh):
    whole = Mesh(np.asarray(mesh.devices).reshape(4, 4, 4, 4, 2), ("x", "l", "y", "h", "k"))
    dp, work = ("x", "l"), ("y", "h", "k")
    return jax.shard_map(
        local,
        mesh=whole,
        in_specs=(P(dp, work), P(dp, work), P(work, None, None), P(), P(None, work)),
        out_specs=(P(None, work), P(None, work), P(dp, work)),
        check_vma=False,
    )
```

```python
import jax
import jax.numpy as jnp
import numpy as np
from jax import lax
from jax.sharding import Mesh, PartitionSpec as P

BF16 = jnp.bfloat16
SHIFTS = (1, 2, 3)


def shifted(value, axis, shift):
    size = lax.axis_size(axis)
    return lax.ppermute(value, axis, [(i, (i + shift) % size) for i in range(size)])


def swapped(value, axis, mask):
    return lax.ppermute(value, axis, [(i, i ^ mask) for i in range(lax.axis_size(axis))])


def contract_rows(first_operand, second_operand):
    return lax.dot_general(
        first_operand, second_operand, (((0,), (0,)), ((), ())), preferred_element_type=jnp.float32
    )


def pick(stacked, index):
    return lax.dynamic_index_in_dim(stacked, index, 0, keepdims=False)


def contract_tokens(stacked, values):
    return jnp.einsum("btf,tc->bfc", stacked, values, preferred_element_type=jnp.float32)


def product(values, matrix):
    return jnp.dot(values, matrix, preferred_element_type=jnp.float32)


def block_order(values, place, levels):
    columns = values.shape[-1]
    values = values.reshape((2,) * levels + (-1, columns))
    for level in range(levels):
        flipped = jnp.flip(values, levels - 1 - level)
        values = jnp.where((place >> level) % 2 == 1, flipped, values)
    return values.reshape(-1, columns)


def together(*values):
    return lax.optimization_barrier(values)


def after(value, *others):
    return together(value, *others)[0]


def exchanged(pieces, axes):
    return lax.all_to_all(pieces, axes, 0, 0, tiled=True)


def to_all(value, axes, members):
    return exchanged(jnp.broadcast_to(value[None], (members,) + value.shape), axes)


def block_panels(side, panel_slot, h, k):
    rows, width = side.shape[1] // 8, side.shape[2]
    side = side.reshape(16, 2, rows, width)
    own = lax.dynamic_index_in_dim(side, k, 1, keepdims=False)
    other = swapped(lax.dynamic_index_in_dim(side, 1 - k, 1, keepdims=False), "k", 1)
    stored = jnp.concatenate([own, other], 0)
    at = (panel_slot // 2 ^ h) + 16 * ((panel_slot + k) % 2)
    ordered = jnp.take(stored, at, axis=0, mode="clip")
    return ordered.reshape(4, 8, rows, width)


def local(activations, gradients, left_panels, panel_slot, right_inverse):
    x, l, h, k = (lax.axis_index(name) for name in ("x", "l", "h", "k"))
    total_tokens = activations.shape[0] * 16
    tokens, width = gradients.shape
    own_width = activations.shape[1]
    place = 2 * (h % 2) + k

    panel = pick(left_panels.reshape(4, -1, own_width), x)
    act_0 = jnp.concatenate([activations, panel], 0)
    act_1 = swapped(act_0, "h", 1)
    act_3 = swapped(act_0, "h", 3)
    act_1, act_3, gradients = together(act_1, act_3, gradients)
    act_2 = swapped(act_1, "h", 3)
    grad_1 = swapped(gradients, "h", 1)
    panels = jnp.concatenate([panel, act_1[tokens:], panel, act_3[tokens:]], 0)
    mine = jnp.concatenate([activations, act_1[:tokens], act_3[:tokens], panels], 1)
    early = to_all(mine, "y", 4)
    grad_other = swapped(gradients, "k", 1)
    mine_other = swapped(mine, "k", 1)
    inverse = block_order(right_inverse, place, 2).reshape(4, width, -1)
    grad_right = product(gradients, inverse[0]) + product(grad_other, inverse[1])
    output_part = [contract_rows(gradients, gradients), contract_rows(grad_other, gradients)]
    input_part = [contract_rows(part, activations) for part in (mine, mine_other)]
    act_2, grad_1, early, grad_right, inverse, output_0, output_1, input_0, input_1 = together(
        act_2, grad_1, early, grad_right, inverse, *output_part, *input_part
    )

    third = to_all(act_2, "y", 4)
    grad_1_other = swapped(grad_1, "k", 1)
    grad_right = grad_right + product(grad_1, inverse[2]) + product(grad_1_other, inverse[3])
    grad_right = grad_right.astype(BF16)
    grad_right = jnp.concatenate([grad_right, swapped(grad_right, "k", 1)], 1)

    terms = contract_tokens(early, grad_right)[:, : 3 * own_width]
    terms = jnp.concatenate([terms, contract_tokens(third[:, :tokens], grad_right)], 1)
    terms, act_2, grad_1, early, third = together(
        terms.astype(BF16), act_2[:tokens], grad_1, early, third
    )
    got = exchanged(terms, "x")

    input_part = [
        jnp.concatenate([part[: 3 * own_width], contract_rows(last, activations)], 0)
        for part, last in ((input_0, act_2), (input_1, swapped(act_2, "k", 1)))
    ]
    input_part = jnp.stack([part.reshape(4, own_width, own_width) for part in input_part], 1)
    input_part = jnp.concatenate([input_part[:2], input_part[3:], input_part[2:3]], 0)
    input_part = block_order(input_part, 2 * h + k, 3)
    output_part = [output_0, output_1, contract_rows(grad_1, gradients)]
    output_part = jnp.stack(output_part + [contract_rows(grad_1_other, gradients)])
    output_part = block_order(output_part, place, 2)
    factors = jnp.concatenate([input_part, output_part], 1).astype(BF16)
    factors = factors.reshape(4, -1, factors.shape[1])
    quarter = pick(factors, l).astype(jnp.float32)
    for shift in SHIFTS:
        sent = pick(factors, (l + shift) % 4)
        quarter = quarter + shifted(sent, "l", shift).astype(jnp.float32)
    quarter = quarter.astype(BF16)

    held = panel.shape[0]
    side = early[..., 3 * own_width :]
    side = jnp.concatenate([side[:, : 2 * held], third[:, tokens:], side[:, 3 * held :]], 1)
    ordered = block_panels(after(side, factors), panel_slot, h, k)
    rows_got = [pick(ordered, x)] + [shifted(pick(ordered, (x + s) % 4), "x", s) for s in SHIFTS]
    got, quarter = together(got, quarter)
    rows_got = jnp.stack(rows_got)
    left = jnp.concatenate([pick(rows_got, (x - (h ^ m)) % 4) for m in (0, 1, 3, 2)], 1)
    left_other = swapped(left, "k", 1)

    quarter = jnp.sum(to_all(quarter, "x", 4).astype(jnp.float32), 0).astype(BF16)
    right_rows = jnp.sum(got.astype(jnp.float32), 0).astype(BF16)
    right_other = swapped(right_rows[:, width:], "k", 1)
    update = contract_tokens(left, right_rows[:, :width]) + contract_tokens(left_other, right_other)
    update = update.astype(BF16).reshape(4, -1, width)
    quarter = jnp.broadcast_to(quarter[None], (4,) + quarter.shape)
    joint = exchanged(jnp.concatenate([update, quarter], 2), "l")
    step_update = jnp.sum(joint[..., :width].astype(jnp.float32), 0).astype(BF16)
    factors = joint[..., width:].reshape(-1, quarter.shape[2]).astype(jnp.float32)
    return factors[:, :own_width] / total_tokens, factors[:, own_width:], step_update


def solution(mesh):
    whole = Mesh(np.asarray(mesh.devices).reshape(4, 4, 4, 4, 2), ("x", "l", "y", "h", "k"))
    dp, work = ("x", "l"), ("y", "h", "k")
    return jax.shard_map(
        local,
        mesh=whole,
        in_specs=(P(dp, work), P(dp, work), P(work, None, None), P(), P(None, work)),
        out_specs=(P(None, work), P(None, work), P(dp, work)),
        check_vma=False,
    )
```
